32 devices in a mesh: dp: 8 (over z, core), fsdp: 4 (over y, x).
Axes of the slice: x: 2, y: 2, z: 4, core: 2. Of those that a mesh axis runs over, the one named last changes fastest.
Arguments:
- activations: bfloat16 [6144, 8192], P(('dp', 'fsdp')), may hold values from -6 to 6
- cotangent: bfloat16 [6144, 4096], P(('dp', 'fsdp')), may hold values from -0.059814453 to 0.059814453
- basis: bfloat16 [8192, 256], P('fsdp'), may hold values from -0.0625 to 0.0625
- first_moment: float32 [4096, 256], P(('dp', 'fsdp')), may hold values from -1.2 to 1.2
- second_moment: float32 [4096, 256], P(('dp', 'fsdp')), may hold values from 0.005 to 0.05
Outputs:
- update: bfloat16 [8192, 4096], P('fsdp', 'dp')
- new_first: float32 [4096, 256], P(('dp', 'fsdp'))
- new_second: float32 [4096, 256], P(('dp', 'fsdp'))
The draws below stay inside these ranges and needn't reach their ends.
All inputs are finite; a program needn't handle non-finite values.
Results may differ from the reference program's by a relative error of at most 0.0052.
Values may be sent and summed in bfloat16 or wider, within the bound.
No kernel may reach another device: no remote copies, remote signals or barrier semaphores. Data moves between devices by JAX's collectives and lax.ppermute only.
A program may use at most 64 MiB of HBM per device.

```python
import math
import jax
import jax.numpy as jnp
from jax import lax

D = 8192
F = 4096
RANK = 256
ADAM_STEP = 10
TOKENS = 6144


def raised(values, rng, source, target, shards_of, factor):
    owner, partner = [(jnp.arange(values.shape[position]) // (values.shape[position] // shards_of)).reshape([-1 if axis == position else 1 for axis in range(values.ndim)]) for position in (source, target)]
    chosen = jax.random.permutation(rng, shards_of)[partner]
    strong = (owner == chosen) | (owner == (partner + shards_of // 2) % shards_of)
    return jnp.where(strong, factor * values, values)


def steps_of(stream_key, dims, shards, smallest, high):
    factor_of, own = 1.0, jax.random.fold_in(stream_key, 6)
    for dim, parts in shards:
        heights = jnp.exp(jax.random.uniform(jax.random.fold_in(own, dim), (parts,), jnp.float32, smallest / len(shards), high / len(shards)))
        factor_of = factor_of * jnp.repeat(heights, dims[dim] // parts).reshape([-1 if axis == dim else 1 for axis in range(len(dims))])
    return factor_of


def bell_draw(rng, dims, deviation, most, shards=(), dtype=jnp.bfloat16):
    array = deviation * jax.random.normal(rng, dims, jnp.float32)
    if shards:
        array = array * steps_of(rng, dims, shards, -0.22, 0.18)
    return jnp.clip(array, -most, most).astype(dtype)


def noise_with(key, dims, width, limit, pieces, heavy, held_as=jnp.bfloat16):
    result = width * jax.random.normal(key, dims, jnp.float32)
    if pieces:
        result = result * steps_of(key, dims, pieces, -0.22, 0.18)
    return jnp.clip(raised(result, jax.random.fold_in(key, 3), *heavy), -limit, limit).astype(held_as)


def setup_inputs(seed: int = 0) -> dict:
    streams_of = jax.random.split(jax.random.key(seed), 6)
    activations = bell_draw(streams_of[0], (TOKENS, D), 1.0, 6.0, ((0, 32),))
    cotangent = noise_with(streams_of[1], (TOKENS, F), 0.01, 0.059814453, ((0, 32),), (0, 1, 32, 2.75))
    basis = bell_draw(streams_of[2], (D, RANK), D ** -0.5, 0.0625, ((0, 4),))
    first_moment = bell_draw(streams_of[3], (F, RANK), 0.2, 1.2, ((0, 32),), jnp.float32)
    second_moment = jnp.clip(jnp.exp(math.log(0.05) - 2.3025851 * jax.random.uniform(streams_of[4], (F, RANK), jnp.float32) ** steps_of(streams_of[4], (F, RANK), ((0, 32),), -0.2, 0.2)), 0.005, 0.05)
    return {"activations": activations, "cotangent": cotangent, "basis": basis, "first_moment": first_moment, "second_moment": second_moment}


def reference(activations, cotangent, basis, first_moment, second_moment):
    projected = jnp.dot(activations, basis, preferred_element_type=jnp.float32).astype(jnp.bfloat16)
    grad = lax.dot_general(cotangent, projected, (((0,), (0,)), ((), ())), preferred_element_type=jnp.float32)
    new_first = 0.9 * first_moment + 0.1 * grad
    new_second = 0.999 * second_moment + 0.001 * grad * grad
    bias_one = 1.0 - 0.9 ** ADAM_STEP
    bias_two = 1.0 - 0.999 ** ADAM_STEP
    step = (new_first / bias_one / (jnp.sqrt(new_second / bias_two) + 1e-08)).astype(jnp.bfloat16)
    update = lax.dot_general(basis, step, (((1,), (1,)), ((), ())), preferred_element_type=jnp.float32)
    return ((16.0 * update).astype(jnp.bfloat16), new_first, new_second)
```

```python
import jax
import jax.numpy as jnp
from jax import lax
from jax.sharding import PartitionSpec as P

ADAM_STEP = 10


def dot(a, b):
    return jnp.dot(a, b, preferred_element_type=jnp.float32)


def solution(mesh):
    dp, fsdp = mesh.shape["dp"], mesh.shape["fsdp"]
    pairs = dp // 2

    def swap(value, across_pairs=0, across_fsdp=0, across_core=0):
        mask = across_pairs * 2 + across_core
        steps = [
            (d * fsdp + f, (d ^ mask) * fsdp + (f ^ across_fsdp))
            for d in range(dp)
            for f in range(fsdp)
        ]
        return lax.ppermute(value, ("dp", "fsdp"), steps)

    def local(activations, cotangent, basis, first_moment, second_moment):
        tokens, depth, rank = activations.shape[0], basis.shape[0], basis.shape[1]
        half, rows = depth // 2, first_moment.shape[0]
        mine, here = lax.axis_index("dp"), lax.axis_index("fsdp")
        core, pair = mine % 2, mine // 2

        part = lax.dynamic_slice(basis, (core * half, 0), (half, rank))
        parts = [part] + [swap(part, across_fsdp=k) for k in range(1, fsdp)]
        shared = [activations, swap(activations, across_core=1)]
        features = jnp.concatenate([cotangent, swap(cotangent, across_core=1)], axis=0)

        features = features.T.reshape(pairs, 2, fsdp, rows, 2 * tokens)
        features = lax.dynamic_index_in_dim(features, core, 1, keepdims=False)
        features = jnp.take(features, jnp.arange(pairs) ^ pair, axis=0)
        features = jnp.take(features, jnp.arange(fsdp) ^ here, axis=1)
        features = features.swapaxes(0, 1)

        projected = []
        for block in shared:
            total = 0.0
            for k, piece in enumerate(parts):
                start = (here ^ k) * depth + core * half
                total += dot(lax.dynamic_slice(block, (0, start), (tokens, half)), piece)
            projected.append(total)
        projected = jnp.concatenate(projected, axis=0)
        other = swap(projected.astype(jnp.bfloat16), across_core=1)
        other = jnp.concatenate([other[tokens:], other[:tokens]], axis=0)
        projected = (projected + other.astype(jnp.float32)).astype(jnp.bfloat16)

        def term(k):
            return dot(features[k].reshape(-1, 2 * tokens), projected).reshape(pairs, rows, rank)

        arrived = [swap(term(k).astype(jnp.bfloat16), across_fsdp=k) for k in range(1, fsdp)]
        plane = term(0)
        for value in arrived:
            plane += value.astype(jnp.float32)
        arrived = [swap(plane[k].astype(jnp.bfloat16), across_pairs=k) for k in range(1, pairs)]
        grad = plane[0]
        for value in arrived:
            grad += value.astype(jnp.float32)

        new_first = 0.9 * first_moment + 0.1 * grad
        new_second = 0.999 * second_moment + 0.001 * grad * grad
        bias_one = 1.0 - 0.9**ADAM_STEP
        bias_two = 1.0 - 0.999**ADAM_STEP
        step = (new_first / bias_one / (jnp.sqrt(new_second / bias_two) + 1e-08)).astype(jnp.bfloat16)
        update = lax.dot_general(
            basis,
            lax.all_gather(step, "fsdp", axis=0, tiled=True),
            (((1,), (1,)), ((), ())),
            preferred_element_type=jnp.float32,
        )
        return ((16.0 * update).astype(jnp.bfloat16), new_first, new_second)

    in_specs = (
        P(("dp", "fsdp"), None),
        P(("dp", "fsdp"), None),
        P("fsdp", None),
        P(("dp", "fsdp"), None),
        P(("dp", "fsdp"), None),
    )
    out_specs = (P("fsdp", "dp"), P(("dp", "fsdp"), None), P(("dp", "fsdp"), None))
    return jax.shard_map(local, mesh=mesh, in_specs=in_specs, out_specs=out_specs, check_vma=False)
```

```python
import functools

import jax
import jax.numpy as jnp
from jax import lax
from jax.experimental import pallas as pl
from jax.experimental.pallas import tpu as pltpu
from jax.sharding import PartitionSpec as P

ADAM_STEP = 10
ANY = pl.BlockSpec(memory_space=pl.ANY)


def dot(a, b):
    return jnp.dot(a, b, preferred_element_type=jnp.float32)


def copy_all(copies):
    for copy in copies:
        copy.start()
    for copy in copies:
        copy.wait()


def halves_kernel(core, source, first, second, sem):
    half = first.shape[0]
    begins = (core[0] * half, (1 - core[0]) * half)
    copy_all(
        [
            pltpu.make_async_copy(source.at[pl.ds(pl.multiple_of(begin, 16), half), :], out, sem.at[i])
            for i, (begin, out) in enumerate(zip(begins, (first, second)))
        ]
    )


def halves_of(basis, core):
    half, rank = basis.shape[0] // 2, basis.shape[1]
    return pl.pallas_call(
        halves_kernel,
        out_shape=[pltpu.VMEM((half, rank), basis.dtype)] * 2,
        in_specs=[pl.BlockSpec(memory_space=pltpu.SMEM), ANY],
        out_specs=[pl.BlockSpec(memory_space=pltpu.VMEM)] * 2,
        scratch_shapes=[pltpu.SemaphoreType.DMA((2,))],
        name="halves",
    )(core.reshape(1), basis)


def pack_kernel(tokens, starts, own, other, *refs):
    outs, sem = refs[:-1], refs[-1]
    copies = []
    for index, out in enumerate(outs):
        columns = pl.ds(pl.multiple_of(starts[index], 128), out.shape[1])
        for side, source in enumerate((own, other)):
            copies.append(
                pltpu.make_async_copy(
                    source.at[:, columns], out.at[pl.ds(side * tokens, tokens), :], sem.at[2 * index + side]
                )
            )
    copy_all(copies)


def pack(own, other, starts, width):
    tokens, count = own.shape[0], len(starts)
    return pl.pallas_call(
        functools.partial(pack_kernel, tokens),
        out_shape=[pltpu.VMEM((2 * tokens, width), own.dtype)] * count,
        in_specs=[pl.BlockSpec(memory_space=pltpu.SMEM), ANY, ANY],
        out_specs=[pl.BlockSpec(memory_space=pltpu.VMEM)] * count,
        scratch_shapes=[pltpu.SemaphoreType.DMA((2 * count,))],
        name="pack_activations",
    )(jnp.stack(starts), own, other)


def turn_kernel(rows, order, own, other, out):
    for index in range(out.shape[0]):
        columns = pl.ds(pl.multiple_of(order[index] * rows, rows), rows)
        out[index] = jnp.concatenate([own[:, columns], other[:, columns]], axis=0).T


def turn(own, other, order, rows):
    tokens, count = own.shape[0], order.shape[0]
    if rows % 128 or tokens % 16:
        both = jnp.concatenate([own, other], axis=0).T
        return jnp.take(both.reshape(-1, rows, 2 * tokens), order, axis=0)
    return pl.pallas_call(
        functools.partial(turn_kernel, rows),
        out_shape=pltpu.VMEM((count, rows, 2 * tokens), own.dtype),
        in_specs=[pl.BlockSpec(memory_space=pltpu.SMEM)] + [pl.BlockSpec(memory_space=pltpu.VMEM)] * 2,
        out_specs=pl.BlockSpec(memory_space=pltpu.VMEM),
        name="turn_cotangent",
    )(order, own, other)


def update_kernel(basis, step, out):
    product = lax.dot_general(
        basis[...], step[...], (((1,), (1,)), ((), ())), preferred_element_type=jnp.float32
    )
    out[...] = (16.0 * product).astype(out.dtype)


def update_of(basis, step):
    depth, rank = basis.shape
    columns, tile = step.shape[0], depth // 4
    basis = pltpu.with_memory_space_constraint(basis, pltpu.VMEM)
    return pl.pallas_call(
        update_kernel,
        out_shape=jax.ShapeDtypeStruct((depth, columns), jnp.bfloat16),
        grid=(4,),
        in_specs=[
            pl.BlockSpec((tile, rank), lambda i: (i, 0)),
            pl.BlockSpec((columns, rank), lambda i: (0, 0)),
        ],
        out_specs=pl.BlockSpec((tile, columns), lambda i: (i, 0)),
        name="update",
    )(basis, step)


def solution(mesh):
    dp, fsdp = mesh.shape["dp"], mesh.shape["fsdp"]
    pairs = dp // 2

    def swap(value, across_pairs=0, across_fsdp=(0, 0), across_core=0):
        mask = across_pairs * 2 + across_core
        steps = [
            (d * fsdp + f, (d ^ mask) * fsdp + (f ^ across_fsdp[d % 2]))
            for d in range(dp)
            for f in range(fsdp)
        ]
        return lax.ppermute(value, ("dp", "fsdp"), steps)

    def local(activations, cotangent, basis, first_moment, second_moment):
        tokens, depth, rank = activations.shape[0], basis.shape[0], basis.shape[1]
        half, rows = depth // 2, first_moment.shape[0]
        mine, here = lax.axis_index("dp"), lax.axis_index("fsdp")
        core, pair = mine % 2, mine // 2

        part, rest = halves_of(basis, core)
        begin = core * half
        parts, starts = [part], [here * depth + begin]
        if fsdp == 4:
            near = here ^ (1 + core)
            parts.append(swap(part, across_fsdp=(1, 2)))
            parts.append(swap(rest, across_fsdp=(1, 2)))
            parts.append(swap(parts[1], across_fsdp=(2, 1)))
            starts += [near * depth + begin, near * depth + half - begin, (here ^ 3) * depth + begin]
        else:
            for k in range(1, fsdp):
                parts.append(swap(part, across_fsdp=(k, k)))
                starts.append((here ^ k) * depth + begin)

        shared = pack(activations, swap(activations, across_core=1), starts, half)
        order = (
            ((jnp.arange(pairs) ^ pair) * 2 + core)[:, None] * fsdp + (jnp.arange(fsdp) ^ here)[None, :]
        )
        order = order.reshape(2, pairs // 2, fsdp).swapaxes(1, 2).reshape(-1)
        features = turn(cotangent, swap(cotangent, across_core=1), order, rows)
        features = features.reshape(2, fsdp, pairs // 2 * rows, 2 * tokens)
        shared, features = lax.optimization_barrier((shared, features))

        projected = 0.0
        for block, piece in zip(shared, parts):
            projected += dot(block, piece)
        other = swap(projected.astype(jnp.bfloat16), across_core=1)
        other = jnp.concatenate([other[tokens:], other[:tokens]], axis=0)
        projected = (projected + other.astype(jnp.float32)).astype(jnp.bfloat16)

        def term(side, k):
            return dot(features[side, k], projected).reshape(pairs // 2, rows, rank)

        order = sorted(range(1, fsdp), key=lambda k: -bin(k).count("1"))
        arrived = {
            side: [swap(term(side, k).astype(jnp.bfloat16), across_fsdp=(k, k)) for k in order] for side in (1, 0)
        }
        arrivals, plane = [], {}
        for side in (1, 0):
            plane[side] = term(side, 0)
            for value in arrived[side]:
                plane[side] += value.astype(jnp.float32)
            for k in range(side * (pairs // 2), (side + 1) * (pairs // 2)):
                if k:
                    value = plane[side][k - side * (pairs // 2)].astype(jnp.bfloat16)
                    arrivals.append(swap(value, across_pairs=k))
        grad = plane[0][0]
        for value in arrivals:
            grad += value.astype(jnp.float32)

        new_first = 0.9 * first_moment + 0.1 * grad
        new_second = 0.999 * second_moment + 0.001 * grad * grad
        bias_one = 1.0 - 0.9**ADAM_STEP
        bias_two = 1.0 - 0.999**ADAM_STEP
        step = (new_first / bias_one / (jnp.sqrt(new_second / bias_two) + 1e-08)).astype(jnp.bfloat16)
        update = update_of(basis, lax.all_gather(step, "fsdp", axis=0, tiled=True))
        return (update, new_first, new_second)

    in_specs = (
        P(("dp", "fsdp"), None),
        P(("dp", "fsdp"), None),
        P("fsdp", None),
        P(("dp", "fsdp"), None),
        P(("dp", "fsdp"), None),
    )
    out_specs = (P("fsdp", "dp"), P(("dp", "fsdp"), None), P(("dp", "fsdp"), None))
    return jax.shard_map(local, mesh=mesh, in_specs=in_specs, out_specs=out_specs, check_vma=False)
```

```python
import functools

import jax
import jax.numpy as jnp
from jax import lax
from jax.experimental import pallas as pl
from jax.experimental.pallas import tpu as pltpu
from jax.sharding import PartitionSpec as P

ADAM_STEP = 10
ANY = pl.BlockSpec(memory_space=pl.ANY)
SMALL = pltpu.CompilerParams(vmem_limit_bytes=8 * 2**20)


def dot(a, b):
    return jnp.dot(a, b, preferred_element_type=jnp.float32)


def copy_all(copies):
    for copy in copies:
        copy.start()
    for copy in copies:
        copy.wait()


def halves_kernel(core, source, first, second, sem):
    half = first.shape[0]
    begins = (core[0] * half, (1 - core[0]) * half)
    copy_all(
        [
            pltpu.make_async_copy(source.at[pl.ds(pl.multiple_of(begin, 16), half), :], out, sem.at[i])
            for i, (begin, out) in enumerate(zip(begins, (first, second)))
        ]
    )


def halves_of(basis, core):
    half, rank = basis.shape[0] // 2, basis.shape[1]
    return pl.pallas_call(
        halves_kernel,
        out_shape=[pltpu.VMEM((half, rank), basis.dtype)] * 2,
        in_specs=[pl.BlockSpec(memory_space=pltpu.SMEM), pl.BlockSpec(memory_space=pltpu.HBM)],
        out_specs=[pl.BlockSpec(memory_space=pltpu.VMEM)] * 2,
        scratch_shapes=[pltpu.SemaphoreType.DMA((2,))],
        name="halves",
        compiler_params=SMALL,
    )(core.reshape(1), basis)


def pack_kernel(tokens, starts, own, other, *refs):
    outs, sem = refs[:-1], refs[-1]
    copies = []
    for index, out in enumerate(outs):
        columns = pl.ds(pl.multiple_of(starts[index], 128), out.shape[1])
        for side, source in enumerate((own, other)):
            copies.append(
                pltpu.make_async_copy(
                    source.at[:, columns], out.at[pl.ds(side * tokens, tokens), :], sem.at[2 * index + side]
                )
            )
    copy_all(copies)


def pack(own, other, starts, width):
    tokens, count = own.shape[0], len(starts)
    return pl.pallas_call(
        functools.partial(pack_kernel, tokens),
        out_shape=[pltpu.VMEM((2 * tokens, width), own.dtype)] * count,
        in_specs=[pl.BlockSpec(memory_space=pltpu.SMEM), ANY, ANY],
        out_specs=[pl.BlockSpec(memory_space=pltpu.VMEM)] * count,
        scratch_shapes=[pltpu.SemaphoreType.DMA((2 * count,))],
        name="pack_activations",
        compiler_params=SMALL,
    )(jnp.stack(starts), own, other)


def turn_kernel(rows, order, own, other, out):
    for index in range(out.shape[0]):
        columns = pl.ds(pl.multiple_of(order[index] * rows, rows), rows)
        out[index] = jnp.concatenate([own[:, columns], other[:, columns]], axis=0).T


def turn(own, other, order, rows):
    tokens, count = own.shape[0], order.shape[0]
    if rows % 128 or tokens % 16:
        both = jnp.concatenate([own, other], axis=0).T
        return jnp.take(both.reshape(-1, rows, 2 * tokens), order, axis=0)
    return pl.pallas_call(
        functools.partial(turn_kernel, rows),
        out_shape=pltpu.VMEM((count, rows, 2 * tokens), own.dtype),
        in_specs=[pl.BlockSpec(memory_space=pltpu.SMEM)] + [pl.BlockSpec(memory_space=pltpu.VMEM)] * 2,
        out_specs=pl.BlockSpec(memory_space=pltpu.VMEM),
        name="turn_cotangent",
        compiler_params=SMALL,
    )(order, own, other)


def update_kernel(tiles, here, basis, *refs):
    steps, (out, held, sem) = refs[:-3], refs[-3:]
    depth, rows = basis.shape[0], steps[0].shape[0]
    tile, copies = depth // tiles, []
    for mask, step in enumerate(steps):
        columns = pl.ds(pl.multiple_of((here[0] ^ mask) * rows, rows), rows)
        turned = step[...].T
        for index in range(tiles):
            part = pl.ds(index * tile, tile)
            held[mask, part, :] = (16.0 * dot(basis[part, :], turned)).astype(out.dtype)
            copies.append(
                pltpu.make_async_copy(held.at[mask, part, :], out.at[part, columns], sem.at[mask * tiles + index])
            )
            copies[-1].start()
    for copy in copies:
        copy.wait()


def update_of(basis, steps, here):
    depth, (rows, rank) = basis.shape[0], steps[0].shape
    if rows % 128:
        step = jnp.take(jnp.stack(steps), jnp.arange(len(steps)) ^ here, axis=0).reshape(-1, rank)
        return (16.0 * dot(basis, step.T)).astype(jnp.bfloat16)
    tiles = 4
    inputs = [pltpu.with_memory_space_constraint(value, pltpu.VMEM) for value in [basis] + steps]
    return pl.pallas_call(
        functools.partial(update_kernel, tiles),
        out_shape=jax.ShapeDtypeStruct((depth, len(steps) * rows), jnp.bfloat16),
        in_specs=[pl.BlockSpec(memory_space=pltpu.SMEM)] + [pl.BlockSpec(memory_space=pltpu.VMEM)] * len(inputs),
        out_specs=ANY,
        scratch_shapes=[
            pltpu.VMEM((len(steps), depth, rows), jnp.bfloat16),
            pltpu.SemaphoreType.DMA((len(steps) * tiles,)),
        ],
        name="update",
        compiler_params=SMALL,
    )(here.reshape(1), *inputs)


def solution(mesh):
    dp, fsdp = mesh.shape["dp"], mesh.shape["fsdp"]
    pairs = dp // 2

    def swap(value, across_pairs=0, across_fsdp=(0, 0), across_core=0):
        mask = across_pairs * 2 + across_core
        steps = [
            (d * fsdp + f, (d ^ mask) * fsdp + (f ^ across_fsdp[d % 2]))
            for d in range(dp)
            for f in range(fsdp)
        ]
        return lax.ppermute(value, ("dp", "fsdp"), steps)

    def local(activations, cotangent, basis, first_moment, second_moment):
        tokens, depth, rank = activations.shape[0], basis.shape[0], basis.shape[1]
        half, rows = depth // 2, first_moment.shape[0]
        mine, here = lax.axis_index("dp"), lax.axis_index("fsdp")
        core, pair = mine % 2, mine // 2

        part, rest = halves_of(basis, core)
        begin = core * half
        parts = [part]
        if fsdp == 4:
            near = here ^ (1 + core)
            parts += [swap(part, across_fsdp=(1, 2)), swap(rest, across_fsdp=(1, 2))]
            starts = [here * depth + begin, near * depth + begin, near * depth + half - begin, (here ^ 3) * depth + begin]
        else:
            parts += [swap(part, across_fsdp=(k, k)) for k in range(1, fsdp)]
            starts = [(here ^ k) * depth + begin for k in range(fsdp)]

        shared = list(pack(activations, swap(activations, across_core=1), starts, half))
        if fsdp == 4:
            parts[1], shared[1] = lax.optimization_barrier((parts[1], shared[1]))
            parts.append(swap(parts[1], across_fsdp=(2, 1)))

        owners = (
            ((jnp.arange(pairs) ^ pair) * 2 + core)[:, None] * fsdp + (jnp.arange(fsdp) ^ here)[None, :]
        )
        owners = owners.reshape(2, pairs // 2, fsdp).swapaxes(1, 2).reshape(-1)
        features = turn(cotangent, swap(cotangent, across_core=1), owners, rows)
        features = features.reshape(2, fsdp, pairs // 2 * rows, 2 * tokens)
        shared[0], features = lax.optimization_barrier((shared[0], features))

        projected = 0.0
        for block, piece in zip(shared, parts):
            projected = lax.optimization_barrier(projected + dot(block, piece))
        other = swap(projected.astype(jnp.bfloat16), across_core=1)
        other = jnp.concatenate([other[tokens:], other[:tokens]], axis=0)
        projected = (projected + other.astype(jnp.float32)).astype(jnp.bfloat16)

        def term(side, k, value):
            return dot(features[side, k].reshape(-1, 2 * tokens), value).reshape(pairs // 2, rows, rank)

        order = sorted(range(1, fsdp), key=lambda k: -bin(k).count("1"))
        arrivals, arrived, plane, value = [], {}, {}, projected
        for side in (1, 0):
            terms = [term(side, k, value).astype(jnp.bfloat16) for k in order]
            arrived[side] = [swap(v, across_fsdp=(k, k)) for k, v in zip(order, terms)]
            value, arrived[side][0] = lax.optimization_barrier((value, arrived[side][0]))
        for side in (1, 0):
            plane[side] = term(side, 0, projected)
            for other in arrived[side]:
                plane[side] += other.astype(jnp.float32)
            for k in range(side * (pairs // 2), (side + 1) * (pairs // 2)):
                if k:
                    block = plane[side][k - side * (pairs // 2)].astype(jnp.bfloat16)
                    arrivals.append(swap(block, across_pairs=k))
        grad = plane[0][0]
        for value in arrivals:
            grad += value.astype(jnp.float32)

        new_first = 0.9 * first_moment + 0.1 * grad
        new_second = 0.999 * second_moment + 0.001 * grad * grad
        bias_one = 1.0 - 0.9**ADAM_STEP
        bias_two = 1.0 - 0.999**ADAM_STEP
        step = (new_first / bias_one / (jnp.sqrt(new_second / bias_two) + 1e-08)).astype(jnp.bfloat16)
        steps = {k: swap(step, across_fsdp=(k, k)) for k in order}
        update = update_of(basis, [step] + [steps[k] for k in range(1, fsdp)], here)
        return (update, new_first, new_second)

    in_specs = (
        P(("dp", "fsdp"), None),
        P(("dp", "fsdp"), None),
        P("fsdp", None),
        P(("dp", "fsdp"), None),
        P(("dp", "fsdp"), None),
    )
    out_specs = (P("fsdp", "dp"), P(("dp", "fsdp"), None), P(("dp", "fsdp"), None))
    return jax.shard_map(local, mesh=mesh, in_specs=in_specs, out_specs=out_specs, check_vma=False)
```

```python
import functools

import jax
import jax.numpy as jnp
from jax import lax
from jax.experimental import pallas as pl
from jax.experimental.pallas import tpu as pltpu
from jax.sharding import PartitionSpec as P

ADAM_STEP = 10
ANY = pl.BlockSpec(memory_space=pl.ANY)
SMALL = pltpu.CompilerParams(vmem_limit_bytes=8 * 2**20)


def dot(a, b):
    return jnp.dot(a, b, preferred_element_type=jnp.float32)


def copy_all(copies):
    for copy in copies:
        copy.start()
    for copy in copies:
        copy.wait()


def pack_kernel(tokens, starts, own, other, *refs):
    outs, sem = refs[:-1], refs[-1]
    copies = []
    for index, out in enumerate(outs):
        columns = pl.ds(pl.multiple_of(starts[index], 128), out.shape[1])
        for side, source in enumerate((own, other)):
            copies.append(
                pltpu.make_async_copy(
                    source.at[:, columns], out.at[pl.ds(side * tokens, tokens), :], sem.at[2 * index + side]
                )
            )
    copy_all(copies)


def pack(own, other, starts, width):
    tokens, count = own.shape[0], len(starts)
    return pl.pallas_call(
        functools.partial(pack_kernel, tokens),
        out_shape=[pltpu.VMEM((2 * tokens, width), own.dtype)] * count,
        in_specs=[pl.BlockSpec(memory_space=pltpu.SMEM), ANY, ANY],
        out_specs=[pl.BlockSpec(memory_space=pltpu.VMEM)] * count,
        scratch_shapes=[pltpu.SemaphoreType.DMA((2 * count,))],
        name="pack_activations",
        compiler_params=SMALL,
    )(jnp.stack(starts), own, other)


def turn_kernel(rows, order, own, other, out):
    for index in range(out.shape[0]):
        columns = pl.ds(pl.multiple_of(order[index] * rows, rows), rows)
        out[index] = jnp.concatenate([own[:, columns], other[:, columns]], axis=0).T


def turn(own, other, order, rows):
    tokens, count = own.shape[0], order.shape[0]
    if rows % 128 or tokens % 16:
        both = jnp.concatenate([own, other], axis=0).T
        return jnp.take(both.reshape(-1, rows, 2 * tokens), order, axis=0)
    return pl.pallas_call(
        functools.partial(turn_kernel, rows),
        out_shape=pltpu.VMEM((count, rows, 2 * tokens), own.dtype),
        in_specs=[pl.BlockSpec(memory_space=pltpu.SMEM)] + [pl.BlockSpec(memory_space=pltpu.VMEM)] * 2,
        out_specs=pl.BlockSpec(memory_space=pltpu.VMEM),
        name="turn_cotangent",
        compiler_params=SMALL,
    )(order, own, other)


def update_kernel(tiles, masks, place, first, second, *refs):
    steps, (out, step, held, sem) = refs[:-4], refs[-4:]
    half, rows = first.shape[0], steps[0].shape[0]
    for mask, block in zip(masks, steps):
        step[pl.ds(pl.multiple_of((place[0] ^ mask) * rows, rows), rows), :] = block[...]
    turned, tile, copies = step[...].T, half // tiles, []
    for side, basis in enumerate((first, second)):
        for index in range(tiles):
            part = pl.ds(index * tile, tile)
            held[side, part, :] = (16.0 * dot(basis[part, :], turned)).astype(out.dtype)
            begin = pl.multiple_of((place[1] ^ side) * half + index * tile, tile)
            copies.append(
                pltpu.make_async_copy(held.at[side, part, :], out.at[pl.ds(begin, tile), :], sem.at[len(copies)])
            )
            copies[-1].start()
    for copy in copies:
        copy.wait()


def update_of(first, second, steps, masks, here, core):
    half, (rows, rank) = first.shape[0], steps[0].shape
    if rows % 128:
        step = jnp.zeros((len(steps), rows, rank), jnp.bfloat16)
        step = step.at[jnp.array(masks) ^ here].set(jnp.stack(steps)).reshape(-1, rank)
        basis = jnp.where(core == 0, jnp.concatenate([first, second]), jnp.concatenate([second, first]))
        return (16.0 * dot(basis, step.T)).astype(jnp.bfloat16)
    tiles = 4
    inputs = [pltpu.with_memory_space_constraint(value, pltpu.VMEM) for value in [first, second] + steps]
    return pl.pallas_call(
        functools.partial(update_kernel, tiles, masks),
        out_shape=jax.ShapeDtypeStruct((2 * half, len(steps) * rows), jnp.bfloat16),
        in_specs=[pl.BlockSpec(memory_space=pltpu.SMEM)] + [pl.BlockSpec(memory_space=pltpu.VMEM)] * len(inputs),
        out_specs=ANY,
        scratch_shapes=[
            pltpu.VMEM((len(steps) * rows, rank), jnp.bfloat16),
            pltpu.VMEM((2, half, len(steps) * rows), jnp.bfloat16),
            pltpu.SemaphoreType.DMA((2 * tiles,)),
        ],
        name="update",
        compiler_params=SMALL,
    )(jnp.stack([here, core]), *inputs)


def solution(mesh):
    dp, fsdp = mesh.shape["dp"], mesh.shape["fsdp"]
    pairs = dp // 2

    def swap(value, across_pairs=0, across_fsdp=(0, 0), across_core=0):
        mask = across_pairs * 2 + across_core
        steps = [
            (d * fsdp + f, (d ^ mask) * fsdp + (f ^ across_fsdp[d % 2]))
            for d in range(dp)
            for f in range(fsdp)
        ]
        return lax.ppermute(value, ("dp", "fsdp"), steps)

    def local(activations, cotangent, basis, first_moment, second_moment):
        tokens, depth, rank = activations.shape[0], basis.shape[0], basis.shape[1]
        half, rows = depth // 2, first_moment.shape[0]
        mine, here = lax.axis_index("dp"), lax.axis_index("fsdp")
        core, pair = mine % 2, mine // 2

        begin = core * half
        part, rest = (lax.dynamic_slice(basis, (at, 0), (half, rank)) for at in (begin, half - begin))
        parts = [part]
        if fsdp == 4:
            near = here ^ (1 + core)
            parts += [swap(part, across_fsdp=(1, 2)), swap(rest, across_fsdp=(1, 2))]
            starts = [here * depth + begin, near * depth + begin, near * depth + half - begin, (here ^ 3) * depth + begin]
        else:
            parts += [swap(part, across_fsdp=(k, k)) for k in range(1, fsdp)]
            starts = [(here ^ k) * depth + begin for k in range(fsdp)]

        shared = list(pack(activations, swap(activations, across_core=1), starts, half))
        if fsdp == 4:
            parts[1], shared[1] = lax.optimization_barrier((parts[1], shared[1]))
            parts.append(swap(parts[1], across_fsdp=(2, 1)))

        owners = (
            ((jnp.arange(pairs) ^ pair) * 2 + core)[:, None] * fsdp + (jnp.arange(fsdp) ^ here)[None, :]
        )
        owners = owners.reshape(2, pairs // 2, fsdp).swapaxes(1, 2).reshape(-1)
        features = turn(cotangent, swap(cotangent, across_core=1), owners, rows)
        features = features.reshape(2, fsdp, pairs // 2 * rows, 2 * tokens)
        shared[0], features = lax.optimization_barrier((shared[0], features))

        projected = 0.0
        for block, piece in zip(shared, parts):
            projected = lax.optimization_barrier(projected + dot(block, piece))
        other = swap(projected.astype(jnp.bfloat16), across_core=1)
        other = jnp.concatenate([other[tokens:], other[:tokens]], axis=0)
        projected = (projected + other.astype(jnp.float32)).astype(jnp.bfloat16)

        def term(side, k, value):
            return dot(features[side, k].reshape(-1, 2 * tokens), value).reshape(pairs // 2, rows, rank)

        masks, middle = range(fsdp - 1, 0, -1), pairs // 2
        arrivals, arrived, plane, value = [], {}, {}, projected
        for side in (1, 0):
            terms = {k: term(side, k, value).astype(jnp.bfloat16) for k in masks}
            arrived[side] = {k: swap(v, across_fsdp=(k, k)) for k, v in terms.items()}
            value, arrived[side][1] = lax.optimization_barrier((value, arrived[side][1]))
        for side in (1, 0):
            plane[side] = term(side, 0, projected)
            for k in masks:
                plane[side] += arrived[side][k].astype(jnp.float32)
        for k in [middle] + [k for k in range(1, pairs) if k != middle]:
            block = plane[k // middle][k % middle].astype(jnp.bfloat16)
            arrivals.append(swap(block, across_pairs=k))
        grad = plane[0][0]
        for value in arrivals:
            grad += value.astype(jnp.float32)

        new_first = 0.9 * first_moment + 0.1 * grad
        new_second = 0.999 * second_moment + 0.001 * grad * grad
        bias_one = 1.0 - 0.9**ADAM_STEP
        bias_two = 1.0 - 0.999**ADAM_STEP
        step = (new_first / bias_one / (jnp.sqrt(new_second / bias_two) + 1e-08)).astype(jnp.bfloat16)
        steps = {k: swap(step, across_fsdp=(k, k)) for k in range(1, fsdp)}
        update = update_of(part, rest, [step] + [steps[k] for k in masks], [0, *masks], here, core)
        return (update, new_first, new_second)

    in_specs = (
        P(("dp", "fsdp"), None),
        P(("dp", "fsdp"), None),
        P("fsdp", None),
        P(("dp", "fsdp"), None),
        P(("dp", "fsdp"), None),
    )
    out_specs = (P("fsdp", "dp"), P(("dp", "fsdp"), None), P(("dp", "fsdp"), None))
    return jax.shard_map(local, mesh=mesh, in_specs=in_specs, out_specs=out_specs, check_vma=False)
```

```python
import functools

import jax
import jax.numpy as jnp
from jax import lax
from jax.experimental import pallas as pl
from jax.experimental.pallas import tpu as pltpu
from jax.sharding import PartitionSpec as P

ADAM_STEP = 10
ANY = pl.BlockSpec(memory_space=pl.ANY)
SMALL = pltpu.CompilerParams(vmem_limit_bytes=8 * 2**20)


def dot(a, b):
    return jnp.dot(a, b, preferred_element_type=jnp.float32)


def copy_all(copies):
    for copy in copies:
        copy.start()
    for copy in copies:
        copy.wait()


def pack_kernel(tokens, starts, own, other, *refs):
    outs, sem = refs[:-1], refs[-1]
    copies = []
    for index, out in enumerate(outs):
        columns = pl.ds(pl.multiple_of(starts[index], 128), out.shape[1])
        for side, source in enumerate((own, other)):
            copies.append(
                pltpu.make_async_copy(
                    source.at[:, columns], out.at[pl.ds(side * tokens, tokens), :], sem.at[2 * index + side]
                )
            )
    copy_all(copies)


def pack(own, other, starts, width):
    tokens, count = own.shape[0], len(starts)
    return pl.pallas_call(
        functools.partial(pack_kernel, tokens),
        out_shape=[pltpu.VMEM((2 * tokens, width), own.dtype)] * count,
        in_specs=[pl.BlockSpec(memory_space=pltpu.SMEM), ANY, ANY],
        out_specs=[pl.BlockSpec(memory_space=pltpu.VMEM)] * count,
        scratch_shapes=[pltpu.SemaphoreType.DMA((2 * count,))],
        name="pack_activations",
        compiler_params=SMALL,
    )(jnp.stack(starts), own, other)


def turn_kernel(rows, order, own, other, out):
    for index in range(out.shape[0]):
        columns = pl.ds(pl.multiple_of(order[index] * rows, rows), rows)
        out[index] = jnp.concatenate([own[:, columns], other[:, columns]], axis=0).T


def turn(own, other, order, rows):
    tokens, count = own.shape[0], order.shape[0]
    if rows % 128 or tokens % 16:
        both = jnp.concatenate([own, other], axis=0).T
        return jnp.take(both.reshape(-1, rows, 2 * tokens), order, axis=0)
    return pl.pallas_call(
        functools.partial(turn_kernel, rows),
        out_shape=pltpu.VMEM((count, rows, 2 * tokens), own.dtype),
        in_specs=[pl.BlockSpec(memory_space=pltpu.SMEM)] + [pl.BlockSpec(memory_space=pltpu.VMEM)] * 2,
        out_specs=pl.BlockSpec(memory_space=pltpu.VMEM),
        name="turn_cotangent",
        compiler_params=SMALL,
    )(order, own, other)


def update_kernel(tiles, masks, place, first, second, *refs):
    steps, (out, step, held, sem) = refs[:-4], refs[-4:]
    half, rows = first.shape[0], steps[0].shape[0]
    for mask, block in zip(masks, steps):
        step[pl.ds(pl.multiple_of((place[0] ^ mask) * rows, rows), rows), :] = block[...]
    turned, tile, copies = step[...].T, half // tiles, []
    for side, basis in enumerate((first, second)):
        for index in range(tiles):
            part = pl.ds(index * tile, tile)
            held[side, part, :] = (16.0 * dot(basis[part, :], turned)).astype(out.dtype)
            begin = pl.multiple_of((place[1] ^ side) * half + index * tile, tile)
            copies.append(
                pltpu.make_async_copy(held.at[side, part, :], out.at[pl.ds(begin, tile), :], sem.at[len(copies)])
            )
            copies[-1].start()
    for copy in copies:
        copy.wait()


def update_of(first, second, steps, masks, here, core):
    half, (rows, rank) = first.shape[0], steps[0].shape
    if rows % 128:
        step = jnp.zeros((len(steps), rows, rank), jnp.bfloat16)
        step = step.at[jnp.array(masks) ^ here].set(jnp.stack(steps)).reshape(-1, rank)
        basis = jnp.where(core == 0, jnp.concatenate([first, second]), jnp.concatenate([second, first]))
        return (16.0 * dot(basis, step.T)).astype(jnp.bfloat16)
    tiles = 4
    inputs = [pltpu.with_memory_space_constraint(value, pltpu.VMEM) for value in [first, second] + steps]
    return pl.pallas_call(
        functools.partial(update_kernel, tiles, masks),
        out_shape=jax.ShapeDtypeStruct((2 * half, len(steps) * rows), jnp.bfloat16),
        in_specs=[pl.BlockSpec(memory_space=pltpu.SMEM)] + [pl.BlockSpec(memory_space=pltpu.VMEM)] * len(inputs),
        out_specs=ANY,
        scratch_shapes=[
            pltpu.VMEM((len(steps) * rows, rank), jnp.bfloat16),
            pltpu.VMEM((2, half, len(steps) * rows), jnp.bfloat16),
            pltpu.SemaphoreType.DMA((2 * tiles,)),
        ],
        name="update",
        compiler_params=SMALL,
    )(jnp.stack([here, core]), *inputs)


def solution(mesh):
    dp, fsdp = mesh.shape["dp"], mesh.shape["fsdp"]
    pairs = dp // 2

    def swap(value, across_pairs=0, across_fsdp=(0, 0), across_core=0):
        mask = across_pairs * 2 + across_core
        steps = [
            (d * fsdp + f, (d ^ mask) * fsdp + (f ^ across_fsdp[d % 2]))
            for d in range(dp)
            for f in range(fsdp)
        ]
        return lax.ppermute(value, ("dp", "fsdp"), steps)

    def local(activations, cotangent, basis, first_moment, second_moment):
        tokens, depth, rank = activations.shape[0], basis.shape[0], basis.shape[1]
        half, rows = depth // 2, first_moment.shape[0]
        mine, here = lax.axis_index("dp"), lax.axis_index("fsdp")
        core, pair = mine % 2, mine // 2

        begin = core * half
        part = lax.dynamic_slice(basis, (begin, 0), (half, rank))
        part, later = lax.optimization_barrier((part, basis))
        rest = lax.dynamic_slice(later, (half - begin, 0), (half, rank))
        parts = [part]
        if fsdp == 4:
            near = here ^ (1 + core)
            parts += [swap(part, across_fsdp=(1, 2)), swap(rest, across_fsdp=(1, 2))]
            starts = [here * depth + begin, near * depth + begin, near * depth + half - begin, (here ^ 3) * depth + begin]
        else:
            parts += [swap(part, across_fsdp=(k, k)) for k in range(1, fsdp)]
            starts = [(here ^ k) * depth + begin for k in range(fsdp)]

        shared = list(pack(activations, swap(activations, across_core=1), starts, half))
        if fsdp == 4:
            parts[1], shared[1] = lax.optimization_barrier((parts[1], shared[1]))
            parts.append(swap(parts[1], across_fsdp=(2, 1)))

        owners = (
            ((jnp.arange(pairs) ^ pair) * 2 + core)[:, None] * fsdp + (jnp.arange(fsdp) ^ here)[None, :]
        )
        owners = owners.reshape(2, pairs // 2, fsdp).swapaxes(1, 2).reshape(-1)
        other, parts[1] = lax.optimization_barrier((swap(cotangent, across_core=1), parts[1]))
        features = turn(cotangent, other, owners, rows)
        features = features.reshape(2, fsdp, pairs // 2 * rows, 2 * tokens)
        shared[0], features = lax.optimization_barrier((shared[0], features))

        projected = 0.0
        for block, piece in zip(shared, parts):
            projected = lax.optimization_barrier(projected + dot(block, piece))
        other = swap(projected.astype(jnp.bfloat16), across_core=1)
        other = jnp.concatenate([other[tokens:], other[:tokens]], axis=0)
        projected = (projected + other.astype(jnp.float32)).astype(jnp.bfloat16)

        def term(side, k, value):
            return dot(features[side, k].reshape(-1, 2 * tokens), value).reshape(pairs // 2, rows, rank)

        masks, middle = range(1, fsdp), pairs // 2
        arrivals, arrived, plane, value = [], {}, {}, projected
        for side in (1, 0):
            terms = {k: term(side, k, value).astype(jnp.bfloat16) for k in masks}
            arrived[side] = {k: swap(v, across_fsdp=(k, k)) for k, v in terms.items()}
            value, arrived[side][1] = lax.optimization_barrier((value, arrived[side][1]))
        for side in (0, 1):
            plane[side] = term(side, 0, projected)
            for k in masks:
                plane[side] += arrived[side][k].astype(jnp.float32)
        for k in [middle] + [k for k in range(1, pairs) if k != middle]:
            block = plane[k // middle][k % middle].astype(jnp.bfloat16)
            arrivals.append(swap(block, across_pairs=k))
        grad = plane[0][0]
        for value in arrivals:
            grad += value.astype(jnp.float32)

        def moments(grad):
            return 0.9 * first_moment + 0.1 * grad, 0.999 * second_moment + 0.001 * grad * grad

        bias_one = 1.0 - 0.9**ADAM_STEP
        bias_two = 1.0 - 0.999**ADAM_STEP
        new_first, new_second = moments(grad)
        step = (new_first / bias_one / (jnp.sqrt(new_second / bias_two) + 1e-08)).astype(jnp.bfloat16)
        step, kept = lax.optimization_barrier((step, grad))
        new_first, new_second = moments(kept)
        steps = {k: swap(step, across_fsdp=(k, k)) for k in masks}
        update = update_of(part, rest, [step] + [steps[k] for k in masks[::-1]], [0, *masks[::-1]], here, core)
        return (update, new_first, new_second)

    in_specs = (
        P(("dp", "fsdp"), None),
        P(("dp", "fsdp"), None),
        P("fsdp", None),
        P(("dp", "fsdp"), None),
        P(("dp", "fsdp"), None),
    )
    out_specs = (P("fsdp", "dp"), P(("dp", "fsdp"), None), P(("dp", "fsdp"), None))
    return jax.shard_map(local, mesh=mesh, in_specs=in_specs, out_specs=out_specs, check_vma=False)
```

```python
import functools

import jax
import jax.numpy as jnp
from jax import lax
from jax.experimental import pallas as pl
from jax.experimental.pallas import tpu as pltpu
from jax.sharding import PartitionSpec as P

ADAM_STEP = 10
ANY = pl.BlockSpec(memory_space=pl.ANY)
SMALL = pltpu.CompilerParams(vmem_limit_bytes=8 * 2**20)


def dot(a, b):
    return jnp.dot(a, b, preferred_element_type=jnp.float32)


def copy_all(copies):
    for copy in copies:
        copy.start()
    for copy in copies:
        copy.wait()


def pack_kernel(tokens, starts, own, other, *refs):
    outs, sem = refs[:-1], refs[-1]
    copies = []
    for index, out in enumerate(outs):
        columns = pl.ds(pl.multiple_of(starts[index], 128), out.shape[1])
        for side, source in enumerate((own, other)):
            copies.append(
                pltpu.make_async_copy(
                    source.at[:, columns], out.at[pl.ds(side * tokens, tokens), :], sem.at[2 * index + side]
                )
            )
    copy_all(copies)


def pack(own, other, starts, width):
    tokens, count = own.shape[0], len(starts)
    return pl.pallas_call(
        functools.partial(pack_kernel, tokens),
        out_shape=[pltpu.VMEM((2 * tokens, width), own.dtype)] * count,
        in_specs=[pl.BlockSpec(memory_space=pltpu.SMEM), ANY, ANY],
        out_specs=[pl.BlockSpec(memory_space=pltpu.VMEM)] * count,
        scratch_shapes=[pltpu.SemaphoreType.DMA((2 * count,))],
        name="pack_activations",
        compiler_params=SMALL,
    )(jnp.stack(starts), own, other)


def turn_kernel(rows, order, own, other, out):
    for index in range(out.shape[0]):
        columns = pl.ds(pl.multiple_of(order[index] * rows, rows), rows)
        out[index] = jnp.concatenate([own[:, columns], other[:, columns]], axis=0).T


def turn(own, other, order, rows):
    tokens, count = own.shape[0], order.shape[0]
    if rows % 128 or tokens % 16:
        both = jnp.concatenate([own, other], axis=0).T
        return jnp.take(both.reshape(-1, rows, 2 * tokens), order, axis=0)
    return pl.pallas_call(
        functools.partial(turn_kernel, rows),
        out_shape=pltpu.VMEM((count, rows, 2 * tokens), own.dtype),
        in_specs=[pl.BlockSpec(memory_space=pltpu.SMEM)] + [pl.BlockSpec(memory_space=pltpu.VMEM)] * 2,
        out_specs=pl.BlockSpec(memory_space=pltpu.VMEM),
        name="turn_cotangent",
        compiler_params=SMALL,
    )(order, own, other)


def update_kernel(tiles, places, first, second, *refs):
    steps, (out, step, held, sem) = refs[:-4], refs[-4:]
    core, owners = places()
    half, rows = first.shape[0], steps[0].shape[0]
    for index, block in enumerate(steps):
        step[pl.ds(pl.multiple_of(owners[index] * rows, rows), rows), :] = block[...]
    turned, tile, copies = step[...].T, half // tiles, []
    for side, basis in enumerate((first, second)):
        for index in range(tiles):
            part = pl.ds(index * tile, tile)
            held[side, part, :] = (16.0 * dot(basis[part, :], turned)).astype(out.dtype)
            begin = pl.multiple_of((core ^ side) * half + index * tile, tile)
            copies.append(
                pltpu.make_async_copy(held.at[side, part, :], out.at[pl.ds(begin, tile), :], sem.at[len(copies)])
            )
            copies[-1].start()
    for copy in copies:
        copy.wait()


def update_of(first, second, steps, places):
    half, (rows, rank) = first.shape[0], steps[0].shape
    if rows % 128:
        core, owners = places()
        step = jnp.zeros((len(steps), rows, rank), jnp.bfloat16)
        step = step.at[jnp.stack(owners)].set(jnp.stack(steps)).reshape(-1, rank)
        basis = jnp.where(core == 0, jnp.concatenate([first, second]), jnp.concatenate([second, first]))
        return (16.0 * dot(basis, step.T)).astype(jnp.bfloat16)
    tiles = 4
    inputs = [pltpu.with_memory_space_constraint(value, pltpu.VMEM) for value in [first, second] + steps]
    return pl.pallas_call(
        functools.partial(update_kernel, tiles, places),
        out_shape=jax.ShapeDtypeStruct((2 * half, len(steps) * rows), jnp.bfloat16),
        in_specs=[pl.BlockSpec(memory_space=pltpu.VMEM)] * len(inputs),
        out_specs=ANY,
        scratch_shapes=[
            pltpu.VMEM((len(steps) * rows, rank), jnp.bfloat16),
            pltpu.VMEM((2, half, len(steps) * rows), jnp.bfloat16),
            pltpu.SemaphoreType.DMA((2 * tiles,)),
        ],
        name="update",
        compiler_params=SMALL,
    )(*inputs)


def solution(mesh):
    dp, fsdp = mesh.shape["dp"], mesh.shape["fsdp"]
    pairs = dp // 2

    def swap(value, across_pairs=0, across_fsdp=(0, 0), across_core=0):
        mask = across_pairs * 2 + across_core
        steps = [
            (d * fsdp + f, (d ^ mask) * fsdp + (f ^ across_fsdp[d % 2]))
            for d in range(dp)
            for f in range(fsdp)
        ]
        return lax.ppermute(value, ("dp", "fsdp"), steps)

    def local(activations, cotangent, basis, first_moment, second_moment):
        tokens, depth, rank = activations.shape[0], basis.shape[0], basis.shape[1]
        half, rows = depth // 2, first_moment.shape[0]
        mine, here = lax.axis_index("dp"), lax.axis_index("fsdp")
        core, pair = mine % 2, mine // 2

        begin = core * half
        part = lax.dynamic_slice(basis, (begin, 0), (half, rank))
        part, later = lax.optimization_barrier((part, basis))
        rest = lax.dynamic_slice(later, (half - begin, 0), (half, rank))
        parts = [part]
        if fsdp == 4:
            near = here ^ (1 + core)
            parts += [swap(part, across_fsdp=(1, 2)), swap(rest, across_fsdp=(1, 2))]
            starts = [here * depth + begin, near * depth + begin, near * depth + half - begin, (here ^ 3) * depth + begin]
        else:
            parts += [swap(part, across_fsdp=(k, k)) for k in range(1, fsdp)]
            starts = [(here ^ k) * depth + begin for k in range(fsdp)]

        shared = list(pack(activations, swap(activations, across_core=1), starts, half))
        if fsdp == 4:
            parts[1], shared[1] = lax.optimization_barrier((parts[1], shared[1]))
            parts.append(swap(parts[1], across_fsdp=(2, 1)))

        hops = {k: (k, k) for k in range(1, fsdp)}
        if fsdp == 4:
            hops[1], hops[2] = (1, 2), (2, 1)

        def home(here, core, k):
            first, second = hops.get(k, (0, 0))
            return here ^ (first + core * (second - first))

        homes = [home(here, core, k) for k in range(fsdp)]
        owners = ((jnp.arange(pairs) ^ pair) * 2 + core)[:, None] * fsdp + jnp.stack(homes)[None, :]
        owners = owners.reshape(2, pairs // 2, fsdp).swapaxes(1, 2).reshape(-1)
        other, parts[1] = lax.optimization_barrier((swap(cotangent, across_core=1), parts[1]))
        features = turn(cotangent, other, owners, rows)
        features = features.reshape(2, fsdp, pairs // 2 * rows, 2 * tokens)
        shared[0], features = lax.optimization_barrier((shared[0], features))

        projected = 0.0
        for block, piece in zip(shared, parts):
            projected = lax.optimization_barrier(projected + dot(block, piece))
        other = swap(projected.astype(jnp.bfloat16), across_core=1)
        other = jnp.concatenate([other[tokens:], other[:tokens]], axis=0)
        projected = (projected + other.astype(jnp.float32)).astype(jnp.bfloat16)

        def term(side, k, value):
            return dot(features[side, k].reshape(-1, 2 * tokens), value).reshape(pairs // 2, rows, rank)

        masks, middle = range(1, fsdp), pairs // 2
        arrivals, arrived, plane, value = [], {}, {}, projected
        for side in (1, 0):
            terms = {k: term(side, k, value).astype(jnp.bfloat16) for k in masks}
            arrived[side] = {k: swap(v, across_fsdp=hops[k]) for k, v in terms.items()}
            value, arrived[side][1] = lax.optimization_barrier((value, arrived[side][1]))
        for side in (0, 1):
            plane[side] = term(side, 0, projected)
            for k in masks:
                plane[side] += arrived[side][k].astype(jnp.float32)
        for k in [middle] + [k for k in range(1, pairs) if k != middle]:
            block = plane[k // middle][k % middle].astype(jnp.bfloat16)
            arrivals.append(swap(block, across_pairs=k))
        grad = plane[0][0]
        for value in arrivals:
            grad += value.astype(jnp.float32)

        def moments(grad):
            return 0.9 * first_moment + 0.1 * grad, 0.999 * second_moment + 0.001 * grad * grad

        bias_one = 1.0 - 0.9**ADAM_STEP
        bias_two = 1.0 - 0.999**ADAM_STEP
        new_first, new_second = moments(grad)
        step = (new_first / bias_one / (jnp.sqrt(new_second / bias_two) + 1e-08)).astype(jnp.bfloat16)
        step, kept = lax.optimization_barrier((step, grad))
        new_first, new_second = moments(kept)
        steps = {k: swap(step, across_fsdp=hops[k]) for k in masks}
        late = [0, *masks[::-1]]

        def places():
            here, core = lax.axis_index("fsdp"), lax.rem(lax.axis_index("dp"), 2)
            return core, [home(here, core, k) for k in late]

        update = update_of(part, rest, [step] + [steps[k] for k in late[1:]], places)
        return (update, new_first, new_second)

    in_specs = (
        P(("dp", "fsdp"), None),
        P(("dp", "fsdp"), None),
        P("fsdp", None),
        P(("dp", "fsdp"), None),
        P(("dp", "fsdp"), None),
    )
    out_specs = (P("fsdp", "dp"), P(("dp", "fsdp"), None), P(("dp", "fsdp"), None))
    return jax.shard_map(local, mesh=mesh, in_specs=in_specs, out_specs=out_specs, check_vma=False)
```

```python
import functools

import jax
import jax.numpy as jnp
from jax import lax
from jax.experimental import pallas as pl
from jax.experimental.pallas import tpu as pltpu
from jax.sharding import PartitionSpec as P

ADAM_STEP = 10
ANY = pl.BlockSpec(memory_space=pl.ANY)
SMALL = pltpu.CompilerParams(vmem_limit_bytes=8 * 2**20)


def dot(a, b):
    return jnp.dot(a, b, preferred_element_type=jnp.float32)


def copy_all(copies):
    for copy in copies:
        copy.start()
    for copy in copies:
        copy.wait()


def pack_kernel(tokens, starts, own, other, *refs):
    outs, sem = refs[:-1], refs[-1]
    copies = []
    for index, out in enumerate(outs):
        columns = pl.ds(pl.multiple_of(starts[index], 128), out.shape[1])
        for side, source in enumerate((own, other)):
            copies.append(
                pltpu.make_async_copy(
                    source.at[:, columns], out.at[pl.ds(side * tokens, tokens), :], sem.at[2 * index + side]
                )
            )
    copy_all(copies)


def pack(own, other, starts, width):
    tokens, count = own.shape[0], len(starts)
    return pl.pallas_call(
        functools.partial(pack_kernel, tokens),
        out_shape=[pltpu.VMEM((2 * tokens, width), own.dtype)] * count,
        in_specs=[pl.BlockSpec(memory_space=pltpu.SMEM), ANY, ANY],
        out_specs=[pl.BlockSpec(memory_space=pltpu.VMEM)] * count,
        scratch_shapes=[pltpu.SemaphoreType.DMA((2 * count,))],
        name="pack_activations",
        compiler_params=SMALL,
    )(jnp.stack(starts), own, other)


def turn_kernel(rows, order, own, other, out):
    for index in range(out.shape[0]):
        columns = pl.ds(pl.multiple_of(order[index] * rows, rows), rows)
        out[index] = jnp.concatenate([own[:, columns], other[:, columns]], axis=0).T


def turn(own, other, order, rows):
    tokens, count = own.shape[0], order.shape[0]
    if rows % 128 or tokens % 16:
        both = jnp.concatenate([own, other], axis=0).T
        return jnp.take(both.reshape(-1, rows, 2 * tokens), order, axis=0)
    return pl.pallas_call(
        functools.partial(turn_kernel, rows),
        out_shape=pltpu.VMEM((count, rows, 2 * tokens), own.dtype),
        in_specs=[pl.BlockSpec(memory_space=pltpu.SMEM)] + [pl.BlockSpec(memory_space=pltpu.VMEM)] * 2,
        out_specs=pl.BlockSpec(memory_space=pltpu.VMEM),
        name="turn_cotangent",
        compiler_params=SMALL,
    )(order, own, other)


def update_kernel(tiles, places, first, second, *refs):
    steps, (out, step, held, sem) = refs[:-4], refs[-4:]
    core, owners = places()
    half, rows = first.shape[0], steps[0].shape[0]
    for index, block in enumerate(steps):
        step[pl.ds(pl.multiple_of(owners[index] * rows, rows), rows), :] = block[...]
    turned, tile, copies = step[...].T, half // tiles, []
    for side, basis in enumerate((first, second)):
        for index in range(tiles):
            part = pl.ds(index * tile, tile)
            held[side, part, :] = (16.0 * dot(basis[part, :], turned)).astype(out.dtype)
            begin = pl.multiple_of((core ^ side) * half + index * tile, tile)
            copies.append(
                pltpu.make_async_copy(held.at[side, part, :], out.at[pl.ds(begin, tile), :], sem.at[len(copies)])
            )
            copies[-1].start()
    for copy in copies:
        copy.wait()


def update_of(first, second, steps, places):
    half, (rows, rank) = first.shape[0], steps[0].shape
    if rows % 128:
        core, owners = places()
        step = jnp.zeros((len(steps), rows, rank), jnp.bfloat16)
        step = step.at[jnp.stack(owners)].set(jnp.stack(steps)).reshape(-1, rank)
        basis = jnp.where(core == 0, jnp.concatenate([first, second]), jnp.concatenate([second, first]))
        return (16.0 * dot(basis, step.T)).astype(jnp.bfloat16)
    tiles = 4
    inputs = [pltpu.with_memory_space_constraint(value, pltpu.VMEM) for value in [first, second] + steps]
    return pl.pallas_call(
        functools.partial(update_kernel, tiles, places),
        out_shape=jax.ShapeDtypeStruct((2 * half, len(steps) * rows), jnp.bfloat16),
        in_specs=[pl.BlockSpec(memory_space=pltpu.VMEM)] * len(inputs),
        out_specs=ANY,
        scratch_shapes=[
            pltpu.VMEM((len(steps) * rows, rank), jnp.bfloat16),
            pltpu.VMEM((2, half, len(steps) * rows), jnp.bfloat16),
            pltpu.SemaphoreType.DMA((2 * tiles,)),
        ],
        name="update",
        compiler_params=SMALL,
    )(*inputs)


def solution(mesh):
    dp, fsdp = mesh.shape["dp"], mesh.shape["fsdp"]
    pairs = dp // 2

    def swap(value, across_pairs=0, across_fsdp=(0, 0), across_core=0):
        mask = across_pairs * 2 + across_core
        steps = [
            (d * fsdp + f, (d ^ mask) * fsdp + (f ^ across_fsdp[d % 2]))
            for d in range(dp)
            for f in range(fsdp)
        ]
        return lax.ppermute(value, ("dp", "fsdp"), steps)

    def local(activations, cotangent, basis, first_moment, second_moment):
        tokens, depth, rank = activations.shape[0], basis.shape[0], basis.shape[1]
        half, rows = depth // 2, first_moment.shape[0]
        mine, here = lax.axis_index("dp"), lax.axis_index("fsdp")
        core, pair = mine % 2, mine // 2

        begin = core * half
        part = lax.dynamic_slice(basis, (begin, 0), (half, rank))
        part, later = lax.optimization_barrier((part, basis))
        rest = lax.dynamic_slice(later, (half - begin, 0), (half, rank))
        parts = [part]
        if fsdp == 4:
            near = here ^ (1 + core)
            parts += [swap(part, across_fsdp=(1, 2)), swap(rest, across_fsdp=(1, 2))]
            starts = [here * depth + begin, near * depth + begin, near * depth + half - begin, (here ^ 3) * depth + begin]
        else:
            parts += [swap(part, across_fsdp=(k, k)) for k in range(1, fsdp)]
            starts = [(here ^ k) * depth + begin for k in range(fsdp)]

        shared = list(pack(activations, swap(activations, across_core=1), starts, half))
        if fsdp == 4:
            parts[1], shared[1] = lax.optimization_barrier((parts[1], shared[1]))
            parts.append(swap(parts[1], across_fsdp=(2, 1)))

        hops = {k: (k, k) for k in range(1, fsdp)}
        if fsdp == 4:
            hops[1], hops[2] = (1, 2), (2, 1)

        def home(here, core, k):
            first, second = hops.get(k, (0, 0))
            return here ^ (first + core * (second - first))

        homes = [home(here, core, k) for k in range(fsdp)]
        owners = ((jnp.arange(pairs) ^ pair) * 2 + core)[:, None] * fsdp + jnp.stack(homes)[None, :]
        owners = owners.reshape(2, pairs // 2, fsdp).swapaxes(1, 2).reshape(-1)
        other, parts[1] = lax.optimization_barrier((swap(cotangent, across_core=1), parts[1]))
        features = turn(cotangent, other, owners, rows)
        features = features.reshape(2, fsdp, pairs // 2 * rows, 2 * tokens)
        shared[0], features = lax.optimization_barrier((shared[0], features))

        projected = 0.0
        for block, piece in zip(shared, parts):
            projected = lax.optimization_barrier(projected + dot(block, piece))
        other = swap(projected.astype(jnp.bfloat16), across_core=1)
        other = jnp.concatenate([other[tokens:], other[:tokens]], axis=0)
        projected = (projected + other.astype(jnp.float32)).astype(jnp.bfloat16)

        def term(side, k, value):
            return dot(features[side, k].reshape(-1, 2 * tokens), value).reshape(pairs // 2, rows, rank)

        masks, middle = list(range(1, fsdp)), pairs // 2
        arrivals, arrived, plane, value = [], {}, {}, projected
        for side in (1, 0):
            terms = {k: term(side, k, value).astype(jnp.bfloat16) for k in masks[::-1]}
            arrived[side] = {k: swap(v, across_fsdp=hops[k]) for k, v in terms.items()}
            value, arrived[side][1] = lax.optimization_barrier((value, arrived[side][1]))
        for side in (1, 0):
            plane[side] = term(side, 0, projected)
            for k in masks[1:] + masks[:1]:
                plane[side] += arrived[side][k].astype(jnp.float32)
        for k in range(1, pairs):
            block = plane[k // middle][k % middle].astype(jnp.bfloat16)
            arrivals.append(swap(block, across_pairs=k))
        grad = plane[0][0]
        for value in arrivals:
            grad += value.astype(jnp.float32)

        def moments(grad):
            return 0.9 * first_moment + 0.1 * grad, 0.999 * second_moment + 0.001 * grad * grad

        bias_one = 1.0 - 0.9**ADAM_STEP
        bias_two = 1.0 - 0.999**ADAM_STEP
        new_first, new_second = moments(grad)
        step = (new_first / bias_one / (jnp.sqrt(new_second / bias_two) + 1e-08)).astype(jnp.bfloat16)
        step, kept = lax.optimization_barrier((step, grad))
        new_first, new_second = moments(kept)
        late = [0, masks[-1], *masks[:-1]]
        steps = {k: swap(step, across_fsdp=hops[k]) for k in late[1:]}

        def places():
            here, core = lax.axis_index("fsdp"), lax.rem(lax.axis_index("dp"), 2)
            return core, [home(here, core, k) for k in late]

        update = update_of(part, rest, [step] + [steps[k] for k in late[1:]], places)
        return (update, new_first, new_second)

    in_specs = (
        P(("dp", "fsdp"), None),
        P(("dp", "fsdp"), None),
        P("fsdp", None),
        P(("dp", "fsdp"), None),
        P(("dp", "fsdp"), None),
    )
    out_specs = (P("fsdp", "dp"), P(("dp", "fsdp"), None), P(("dp", "fsdp"), None))
    return jax.shard_map(local, mesh=mesh, in_specs=in_specs, out_specs=out_specs, check_vma=False)
```
